128 devices in a mesh: int: 16 (over y, x_lo, core), occ: 4 (over z), red: 2 (over x_hi).
Axes of the slice: x: 4 (x_hi: 2, x_lo: 2; x = x_hi * 2 + x_lo), y: 4, z: 4, core: 2. Of those that a mesh axis runs over, the one named last changes fastest.
Arguments:
- amplitudes: bfloat16 [4096, 12800], P('occ', ('red', 'int')), may hold values from -6 to 6
- integrals: bfloat16 [12800, 25600], P('red', 'int'), may hold values from -0.0546875 to 0.0546875
Outputs:
- ladder: bfloat16 [4096, 25600], P('occ', ('int', 'red'))
The draws below stay inside these ranges and needn't reach their ends.
All inputs are finite; a program needn't handle non-finite values.
Results may differ from the reference program's by a relative error of at most 0.015.
Values may be sent and summed in bfloat16 or wider, within the bound.
A program may use at most 192 MiB of HBM per device.

```python
import jax
import jax.numpy as jnp

NV = 3200
OW = 64
AW = 8
PAIRS = 4096
CD = 12800
AB = 25600


def block_levels(rng, shape, pieces, smallest, top_value):
    factor_of, own = 1.0, jax.random.fold_in(rng, 6)
    for dim, parts in pieces:
        heights = jnp.exp(jax.random.uniform(jax.random.fold_in(own, dim), (parts,), jnp.float32, smallest / len(pieces), top_value / len(pieces)))
        factor_of = factor_of * jnp.repeat(heights, shape[dim] // parts).reshape([-1 if axis == dim else 1 for axis in range(len(shape))])
    return factor_of


def gaussian(key, dims, width, bound, split=(), kind=jnp.bfloat16):
    drawn = width * jax.random.normal(key, dims, jnp.float32)
    if split:
        drawn = drawn * block_levels(key, dims, split, -0.22, 0.18)
    return jnp.clip(drawn, -bound, bound).astype(kind)


def setup_inputs(seed: int = 0) -> dict:
    key_of = jax.random.split(jax.random.key(seed), 3)
    amplitudes = gaussian(key_of[0], (PAIRS, CD), 1.0, 6.0, ((0, 4), (1, 32)))
    integrals = gaussian(key_of[1], (CD, AB), CD ** -0.5, 0.0546875, ((0, 2), (1, 16)))
    return dict(amplitudes=amplitudes, integrals=integrals)


def reference(amplitudes, integrals):
    contracted = jnp.dot(amplitudes, integrals, preferred_element_type=jnp.float32)
    cube = contracted.reshape(OW, OW, AW * NV)
    ladder = cube - jnp.transpose(cube, (1, 0, 2))
    return ladder.reshape(OW * OW, AW * NV).astype(jnp.bfloat16)
```

```python
import functools

import jax
import jax.numpy as jnp
from jax import lax
from jax.experimental import pallas as pl
from jax.experimental.pallas import tpu as pltpu
from jax.sharding import PartitionSpec as P

MESH = pl.DeviceIdType.MESH
F32, BF16, I32 = jnp.float32, jnp.bfloat16, jnp.int32

LANES = 128
CHUNK = 400
GROUP = 1600
WINDOW = 1664
HALF = 800
OCC = 1024
DZ = (1, 3, 2, 0)
MIRROR = (1, 0, 2)
DY = (0, 1, 3, 2)
STAGES = ((3, 0), (1, 2))


def dot(a, b, dims=((1,), (0,))):
    return lax.dot_general(a, b, (dims, ((), ())), preferred_element_type=F32)


def kernel(
    t_hbm, v_hbm, out, tv, vv, sel, own, zs, zr, at, acc, rs, rr, lad,
    load_sem, zs_sem, zr_sem, as_sem, ar_sem, rs_sem, rr_sem, ls_sem, lr_sem,
):
    index, z, xh = lax.axis_index("int"), lax.axis_index("occ"), lax.axis_index("red")
    y, xl, c = index // 4, (index // 2) % 2, index % 2

    def device(dy=0, flip_x=0, flip_c=0, dz=0, flip_red=0):
        there = ((y + dy) % 4) * 4 + (xl ^ flip_x) * 2 + (c ^ flip_c)
        return {"int": there, "occ": (z + dz) % 4, "red": xh ^ flip_red}

    load_t = pltpu.make_async_copy(t_hbm, tv, load_sem.at[0])
    load_v = pltpu.make_async_copy(v_hbm, vv, load_sem.at[1])
    load_t.start()
    load_v.start()

    barrier = pltpu.get_barrier_semaphore()
    partners = [device(dy=1), device(dy=2), device(dy=3), device(dz=1), device(dz=2), device(dz=3)]
    partners += [device(flip_x=1), device(flip_c=1), device(flip_red=1)]
    for partner in partners:
        pl.semaphore_signal(barrier, inc=1, device_id=partner, device_id_type=MESH)

    pair = lax.broadcasted_iota(I32, (1, LANES), 1)
    row = lax.broadcasted_iota(I32, (OCC, LANES), 0)

    def pairs_of(owner_is_lower):
        a = jnp.where(owner_is_lower, pair >> 4, pair >> 3)
        b = jnp.where(owner_is_lower, pair & 15, 8 + (pair & 7))
        return a, b

    for b in range(3):
        other = (z + DZ[b]) % 4
        p, q = pairs_of(z < other)
        sel[b] = jnp.where(row == p * 64 + other * 16 + q, 1.0, 0.0).astype(BF16)
        p, q = pairs_of(other < z)
        sel[4 + b] = jnp.where(row == q * 64 + other * 16 + p, -1.0, 0.0).astype(BF16)
    p = pair & 15
    q = (p + 1 + (pair >> 4)) & 15
    plus = jnp.where(pair < 120, p * 64 + z * 16 + q, -1)
    minus = jnp.where(pair < 120, q * 64 + z * 16 + p, -1)
    sel[3] = (jnp.where(row == plus, 1.0, 0.0) - jnp.where(row == minus, 1.0, 0.0)).astype(BF16)

    for b in range(4):
        for g in range(4):
            start = GROUP if g % 2 == 0 else 0
            at[b, g, start : start + WINDOW - GROUP, :] = jnp.zeros((WINDOW - GROUP, LANES), BF16)

    pl.semaphore_wait(barrier, len(partners))
    load_t.wait()

    sends = []

    def send(src, dst, send_sem, recv_sem, to):
        copy = pltpu.make_async_remote_copy(
            src_ref=src, dst_ref=dst, send_sem=send_sem, recv_sem=recv_sem, device_id=to, device_id_type=MESH
        )
        copy.start()
        sends.append(copy)

    def landed(ref, recv_sem):
        pltpu.make_async_copy(ref, ref, recv_sem).wait()

    def chunk(b, dy, rel):
        g = (y + dy) % 4
        start = 64 * (g % 2) + CHUNK * ((xl ^ (rel >> 1)) * 2 + (c ^ (rel & 1)))
        return at.at[b, g, pl.ds(pl.multiple_of(start, 16), CHUNK), :]

    def pass_on(b, n, dy, rel, to_dy, to_rel, to):
        ref = chunk(b, dy, rel)
        send(ref, ref, as_sem.at[b, n], ar_sem.at[b, to_dy, to_rel], to)

    def along_y(b, n, rel):
        for k, dy in enumerate((1, 3, 2)):
            pass_on(b, n + k, 0, rel, (-dy) % 4, rel, device(dy=dy))

    def send_own(b):
        pass_on(b, 0, 0, 0, 0, 2, device(flip_x=1))
        along_y(b, 1, 0)
        pass_on(b, 4, 0, 0, 0, 1, device(flip_c=1))

    def send_neighbours(b):
        landed(chunk(b, 0, 2), ar_sem.at[b, 0, 2])
        along_y(b, 5, 2)
        pass_on(b, 8, 0, 2, 0, 3, device(flip_c=1))

    def share(b, dy):
        for k, rel in enumerate((0, 2)):
            landed(chunk(b, dy, rel), ar_sem.at[b, dy, rel])
            pass_on(b, 9 + 2 * (dy - 1) + k, dy, rel, dy, rel + 1, device(flip_c=1))

    for b in range(3):
        zs[b] = dot(tv[...], sel[4 + b]).astype(BF16)
        send(zs.at[b], zr.at[MIRROR[b]], zs_sem.at[b], zr_sem.at[MIRROR[b]], device(dz=DZ[b]))

    order = [b for stage in STAGES for b in stage]
    here = pl.ds(pl.multiple_of(64 * (y % 2) + CHUNK * (xl * 2 + c), 16), CHUNK)
    for b in range(4):
        own[b] = dot(tv[...], sel[b])
    for b in order:
        if b < 3:
            landed(zr.at[b], zr_sem.at[b])
            at[b, y, here, :] = (own[b] + zr[b].astype(F32)).astype(BF16)
        else:
            at[b, y, here, :] = own[b].astype(BF16)
        send_own(b)
    for b in order:
        send_neighbours(b)

    load_v.wait()

    mine = pl.ds(pl.multiple_of(xh * HALF, 16), HALF)
    theirs = pl.ds(pl.multiple_of((1 - xh) * HALF, 16), HALF)

    def finish(stage):
        for k, b in enumerate(STAGES[stage]):
            landed(rr.at[b], rr_sem.at[b])
            lanes = slice(k * LANES, (k + 1) * LANES)
            lad[b] = (acc[stage, mine, lanes] + rr[b].astype(F32)).astype(BF16)
            if b < 3:
                m = MIRROR[b]
                send(lad.at[b], lad.at[4 + m], ls_sem.at[b], lr_sem.at[m], device(dz=DZ[b]))

    events = [(s, dy) for s in range(len(STAGES)) for dy in DY]
    for n, (s, dy) in enumerate(events):
        if n + 1 < len(events):
            s_next, dy_next = events[n + 1]
            if dy_next:
                for b in STAGES[s_next]:
                    share(b, dy_next)
        for b in STAGES[s]:
            for rel in (1, 3):
                landed(chunk(b, dy, rel), ar_sem.at[b, dy, rel])
        g = (y + dy) % 4
        window = pl.ds(pl.multiple_of(g * GROUP - 64 * (g % 2), 128), WINDOW)
        amplitudes = jnp.concatenate([at[b, g] for b in STAGES[s]], axis=1)
        for half in (theirs, mine):
            product = dot(vv[half, window], amplitudes)
            total = product if dy == DY[0] else acc[s, half, :] + product
            if dy == DY[-1] and half is theirs:
                for k, b in enumerate(STAGES[s]):
                    rs[b] = total[:, k * LANES : (k + 1) * LANES].astype(BF16)
                    send(rs.at[b], rr.at[b], rs_sem.at[b], rr_sem.at[b], device(flip_red=1))
            else:
                acc[s, half, :] = total
        if dy == DY[1] and s > 0:
            finish(s - 1)
    finish(len(STAGES) - 1)

    for b in range(3):
        landed(lad.at[4 + b], lr_sem.at[b])
    parts = jnp.concatenate([lad[b] for b in range(7)], axis=1)
    for n in range(0, OCC, 256):
        places = jnp.concatenate([sel[b, n : n + 256, :] for b in range(7)], axis=1)
        out[:, n : n + 256] = dot(parts, places, ((1,), (1,))).astype(BF16)

    for copy in sends:
        copy.wait_send()


def on_device(amplitudes, integrals):
    dma = pltpu.SemaphoreType.DMA
    stages = len(STAGES)
    width = max(len(stage) for stage in STAGES) * LANES
    ladder = pl.pallas_call(
        kernel,
        out_shape=jax.ShapeDtypeStruct((HALF, OCC), BF16),
        in_specs=[pl.BlockSpec(memory_space=pl.ANY)] * 2,
        out_specs=pl.BlockSpec(memory_space=pltpu.VMEM),
        scratch_shapes=[
            pltpu.VMEM((CHUNK, OCC), BF16),
            pltpu.VMEM((2 * HALF, 4 * GROUP), BF16),
            pltpu.VMEM((7, OCC, LANES), BF16),
            pltpu.VMEM((4, CHUNK, LANES), F32),
            pltpu.VMEM((3, CHUNK, LANES), BF16),
            pltpu.VMEM((3, CHUNK, LANES), BF16),
            pltpu.VMEM((4, 4, WINDOW, LANES), BF16),
            pltpu.VMEM((stages, 2 * HALF, width), F32),
            pltpu.VMEM((4, HALF, LANES), BF16),
            pltpu.VMEM((4, HALF, LANES), BF16),
            pltpu.VMEM((7, HALF, LANES), BF16),
            dma((2,)), dma((3,)), dma((3,)), dma((4, 15)), dma((4, 4, 4)), dma((4,)), dma((4,)), dma((3,)), dma((3,)),
        ],
        compiler_params=pltpu.CompilerParams(
            collective_id=0, has_side_effects=True, vmem_limit_bytes=52 * 2**20
        ),
        name="ladder",
    )(amplitudes.T, integrals.T)
    return ladder.T


def solution(mesh):
    placed = (P("occ", ("red", "int")), P("red", "int"))
    return jax.shard_map(
        on_device, mesh=mesh, in_specs=placed, out_specs=P("occ", ("int", "red")), check_vma=False
    )
```

```python
import functools

import jax
import jax.numpy as jnp
from jax import lax
from jax.experimental import pallas as pl
from jax.experimental.pallas import tpu as pltpu
from jax.sharding import PartitionSpec as P

MESH = pl.DeviceIdType.MESH
F32, BF16, I32 = jnp.float32, jnp.bfloat16, jnp.int32

LANES = 128
CHUNK = 400
GROUP = 1600
SLAB = 1280
HALF = 800
PART = 400
OCC = 1024
DZ = (1, 3, 2, 0)
MIRROR = (1, 0, 2)
DIAG = 3


def dot(a, b, dims=((1,), (0,))):
    return lax.dot_general(a, b, (dims, ((), ())), preferred_element_type=F32)


def kernel(
    t_hbm, v_hbm, out, tv, vv, slabs, sel, own, zs, zr, at, acc, total, rs, rr, lad,
    load_sem, zs_sem, zr_sem, as_sem, ar_sem, ds_sem, dr_sem, rs_sem, rr_sem, ls_sem, lr_sem,
):
    index, z, xh = lax.axis_index("int"), lax.axis_index("occ"), lax.axis_index("red")
    y, xl, c = index // 4, (index // 2) % 2, index % 2

    def device(dy=0, flip_x=0, flip_c=0, dz=0, flip_red=0):
        there = ((y + dy) % 4) * 4 + (xl ^ flip_x) * 2 + (c ^ flip_c)
        return {"int": there, "occ": (z + dz) % 4, "red": xh ^ flip_red}

    load_t = pltpu.make_async_copy(t_hbm, tv, load_sem.at[0])
    load_v = [
        pltpu.make_async_copy(v_hbm.at[:, n * SLAB : (n + 1) * SLAB], slabs.at[n % 2], load_sem.at[1 + n % 2])
        for n in range(4 * GROUP // SLAB)
    ]
    load_t.start()
    load_v[0].start()
    load_v[1].start()

    barrier = pltpu.get_barrier_semaphore()
    partners = [device(dy=1), device(dy=3), device(dz=1), device(dz=2), device(dz=3)]
    partners += [device(flip_x=1), device(flip_c=1), device(flip_red=1)]
    for partner in partners:
        pl.semaphore_signal(barrier, inc=1, device_id=partner, device_id_type=MESH)

    pair = lax.broadcasted_iota(I32, (1, LANES), 1)
    row = lax.broadcasted_iota(I32, (OCC, LANES), 0)

    def pairs_of(owner_is_lower):
        a = jnp.where(owner_is_lower, pair >> 4, pair >> 3)
        b = jnp.where(owner_is_lower, pair & 15, 8 + (pair & 7))
        return a, b

    def select_kept(b):
        other = (z + DZ[b]) % 4
        p, q = pairs_of(z < other)
        sel[b] = jnp.where(row == p * 64 + other * 16 + q, 1.0, 0.0).astype(BF16)

    def select_given(b):
        other = (z + DZ[b]) % 4
        p, q = pairs_of(other < z)
        sel[4 + b] = jnp.where(row == q * 64 + other * 16 + p, -1.0, 0.0).astype(BF16)

    def select_diagonal():
        p = pair & 15
        q = (p + 1 + (pair >> 4)) & 15
        plus = jnp.where(pair < 120, p * 64 + z * 16 + q, -1)
        minus = jnp.where(pair < 120, q * 64 + z * 16 + p, -1)
        sel[DIAG] = (jnp.where(row == plus, 1.0, 0.0) - jnp.where(row == minus, 1.0, 0.0)).astype(BF16)

    def turn(n):
        load_v[n].wait()

        def lanes(k, carry):
            first = pl.multiple_of(k * 128, 128)
            vv[pl.ds(n * SLAB + first, 128), :] = slabs[n % 2, :, pl.ds(first, 128)].T
            return carry

        lax.fori_loop(0, SLAB // 128, lanes, 0, unroll=2)
        if n + 2 < len(load_v):
            load_v[n + 2].start()

    sends = []

    def send(src, dst, send_sem, recv_sem, to):
        copy = pltpu.make_async_remote_copy(
            src_ref=src, dst_ref=dst, send_sem=send_sem, recv_sem=recv_sem, device_id=to, device_id_type=MESH
        )
        copy.start()
        sends.append(copy)

    def landed(ref, recv_sem):
        pltpu.make_async_copy(ref, ref, recv_sem).wait()

    def chunk(b, dy, rel, part=None):
        g = (y + dy) % 4
        start = CHUNK * ((xl ^ (rel >> 1)) * 2 + (c ^ (rel & 1)))
        first, rows = (0, CHUNK) if part is None else (part * 208, 208 - 16 * part)
        return at.at[b, g, pl.ds(pl.multiple_of(start + first, 16), rows), :]

    def pass_on(b, n, dy, rel, to_dy, to_rel, to):
        ref = chunk(b, dy, rel)
        send(ref, ref, as_sem.at[b, n], ar_sem.at[b, to_dy, to_rel], to)

    here = pl.ds(pl.multiple_of(CHUNK * (xl * 2 + c), 16), CHUNK)

    def to_next(b, rel):
        pass_on(b, 1 + 4 * (rel // 2), 0, rel, 3, rel, device(dy=1))

    def to_previous(b, rel):
        pass_on(b, 2 + 4 * (rel // 2), 0, rel, 1, rel, device(dy=3))

    def to_neighbours(b):
        pass_on(b, 0, 0, 0, 0, 2, device(flip_x=1))
        pass_on(b, 3, 0, 0, 0, 1, device(flip_c=1))

    def from_x(b, dy=0):
        landed(chunk(b, dy, 2), ar_sem.at[b, dy, 2])
        pass_on(b, 4 if dy == 0 else 8 + 2 * (dy - 1), dy, 2, dy, 3, device(flip_c=1))

    def share(b, dy, rel):
        landed(chunk(b, dy, rel), ar_sem.at[b, dy, rel])
        pass_on(b, 7 + 2 * (dy - 1) + rel // 2, dy, rel, dy, rel + 1, device(flip_c=1))

    def forward_next(b):
        pass_on(b, 13, 3, 0, 2, 0, device(dy=1))

    def forward_previous(b):
        pass_on(b, 14, 1, 2, 2, 2, device(dy=3))

    def across(dy):
        pass_on(DIAG, (13, 5, 6)[dy - 1], dy, 0, dy, 2, device(flip_x=1))

    def forward_diagonal(dy, k, to):
        ref = chunk(DIAG, dy, 0, k)
        send(ref, ref, ds_sem.at[k], dr_sem.at[k], to)

    def share_diagonal():
        for k in range(2):
            landed(chunk(DIAG, 2, 0, k), dr_sem.at[k])
        across(2)
        pass_on(DIAG, 9, 2, 0, 2, 1, device(flip_c=1))

    mine = xh * HALF
    theirs = (1 - xh) * HALF

    def multiply(b, dy):
        for rel in (1, 3):
            landed(chunk(b, dy, rel), ar_sem.at[b, dy, rel])
        g = (y + dy) % 4
        rows = pl.ds(pl.multiple_of(g * GROUP, 16), GROUP)
        product = dot(at[b, g].T, vv[rows, :])
        if dy == 0:
            acc[b] = product
        elif dy != 2:
            acc[b] += product
        else:
            total[b] = (acc[b] + product).T
            for h in range(2):
                rs[b, h] = total[b, pl.ds(pl.multiple_of(theirs + h * PART, 16), PART), :].astype(BF16)
                if b != DIAG:
                    reduce(b, h)

    def reduce(b, h):
        send(rs.at[b, h], rr.at[b, h], rs_sem.at[b, h], rr_sem.at[b, h], device(flip_red=1))

    def finish(b, h):
        landed(rr.at[b, h], rr_sem.at[b, h])
        rows = pl.ds(pl.multiple_of(mine + h * PART, 16), PART)
        lad[b, h] = (total[b, rows, :] + rr[b, h].astype(F32)).astype(BF16)
        if b != DIAG:
            m = MIRROR[b]
            send(lad.at[b, h], lad.at[4 + m, h], ls_sem.at[b, h], lr_sem.at[m, h], device(dz=DZ[b]))

    select_diagonal()
    for b in range(3):
        select_given(b)
    load_t.wait()
    picked = dot(tv[...], jnp.concatenate([sel[b] for b in range(3, 7)], axis=1)).astype(BF16)
    at[DIAG, y, here, :] = picked[:, :LANES]
    for b in range(3):
        zs[b] = picked[:, (1 + b) * LANES : (2 + b) * LANES]
    pl.semaphore_wait(barrier, len(partners))
    def give(b):
        send(zs.at[b], zr.at[MIRROR[b]], zs_sem.at[b], zr_sem.at[MIRROR[b]], device(dz=DZ[b]))

    give(0)
    give(1)
    to_neighbours(DIAG)
    to_next(DIAG, 0)
    to_previous(DIAG, 0)

    for b in range(3):
        select_kept(b)
    own[...] = dot(tv[...], jnp.concatenate([sel[b] for b in range(3)], axis=1))

    def antisymmetric(b):
        landed(zr.at[b], zr_sem.at[b])
        lanes = slice(b * LANES, (b + 1) * LANES)
        at[b, y, here, :] = (own[:, lanes] + zr[b].astype(F32)).astype(BF16)
        to_neighbours(b)

    turn(0)
    turn(1)
    share(DIAG, 3, 0)
    forward_diagonal(3, 0, device(dy=1))
    share(DIAG, 1, 0)
    forward_diagonal(1, 1, device(dy=3))
    from_x(DIAG)
    antisymmetric(0)
    to_next(0, 0)
    to_previous(0, 0)
    antisymmetric(1)
    to_next(1, 0)
    to_previous(1, 0)
    give(2)
    turn(2)
    turn(3)
    antisymmetric(2)
    across(1)
    across(3)
    share_diagonal()
    turn(4)
    from_x(0)
    to_previous(0, 2)
    to_next(0, 2)
    share(0, 3, 0)
    forward_next(0)
    share(0, 1, 0)
    multiply(DIAG, 0)
    multiply(0, 0)
    from_x(1)
    to_previous(1, 2)
    to_next(1, 2)
    share(1, 3, 0)
    forward_next(1)
    share(1, 1, 0)
    multiply(1, 0)
    from_x(2)
    to_next(2, 0)
    share(0, 1, 2)
    forward_previous(0)
    share(0, 3, 2)
    multiply(2, 0)
    multiply(0, 1)
    share(1, 1, 2)
    forward_previous(1)
    to_previous(2, 2)
    to_previous(2, 0)
    to_next(2, 2)
    share(0, 2, 0)
    from_x(DIAG, 1)
    multiply(0, 3)
    multiply(DIAG, 1)
    share(1, 3, 2)
    share(0, 2, 2)
    from_x(DIAG, 3)
    multiply(1, 1)
    multiply(0, 2)
    from_x(DIAG, 2)
    share(1, 2, 0)
    share(1, 2, 2)
    multiply(1, 3)
    multiply(DIAG, 3)
    share(2, 3, 0)
    forward_next(2)
    share(2, 1, 2)
    forward_previous(2)
    multiply(1, 2)
    multiply(DIAG, 2)
    share(2, 3, 2)
    share(2, 1, 0)
    multiply(2, 1)
    multiply(2, 3)
    share(2, 2, 0)
    share(2, 2, 2)
    finish(0, 0)
    finish(0, 1)
    multiply(2, 2)
    reduce(DIAG, 0)
    reduce(DIAG, 1)
    finish(1, 0)
    finish(1, 1)
    finish(2, 0)
    finish(2, 1)
    for h in range(2):
        finish(DIAG, h)
        for b in range(3):
            landed(lad.at[4 + b, h], lr_sem.at[b, h])
        parts = jnp.concatenate([lad[b, h] for b in range(7)], axis=1)
        for n in range(0, OCC, 256):
            places = jnp.concatenate([sel[b, n : n + 256, :] for b in range(7)], axis=1)
            out[h * PART : (h + 1) * PART, n : n + 256] = dot(parts, places, ((1,), (1,))).astype(BF16)

    for copy in sends:
        copy.wait_send()


def on_device(amplitudes, integrals):
    dma = pltpu.SemaphoreType.DMA
    ladder = pl.pallas_call(
        kernel,
        out_shape=jax.ShapeDtypeStruct((HALF, OCC), BF16),
        in_specs=[pl.BlockSpec(memory_space=pltpu.HBM)] * 2,
        out_specs=pl.BlockSpec(memory_space=pltpu.VMEM),
        scratch_shapes=[
            pltpu.VMEM((CHUNK, OCC), BF16),
            pltpu.VMEM((4 * GROUP, 2 * HALF), BF16),
            pltpu.VMEM((2, 2 * HALF, SLAB), BF16),
            pltpu.VMEM((7, OCC, LANES), BF16),
            pltpu.VMEM((CHUNK, 3 * LANES), F32),
            pltpu.VMEM((3, CHUNK, LANES), BF16),
            pltpu.VMEM((3, CHUNK, LANES), BF16),
            pltpu.VMEM((4, 4, GROUP, LANES), BF16),
            pltpu.VMEM((4, LANES, 2 * HALF), F32),
            pltpu.VMEM((4, 2 * HALF, LANES), F32),
            pltpu.VMEM((4, 2, PART, LANES), BF16),
            pltpu.VMEM((4, 2, PART, LANES), BF16),
            pltpu.VMEM((7, 2, PART, LANES), BF16),
            dma((3,)), dma((3,)), dma((3,)), dma((4, 15)), dma((4, 4, 4)), dma((2,)), dma((2,)),
            dma((4, 2)), dma((4, 2)), dma((3, 2)), dma((3, 2)),
        ],
        compiler_params=pltpu.CompilerParams(
            collective_id=0, has_side_effects=True, vmem_limit_bytes=60 * 2**20
        ),
        name="ladder",
    )(amplitudes.T, integrals.T)
    return ladder.T


def solution(mesh):
    placed = (P("occ", ("red", "int")), P("red", "int"))
    return jax.shard_map(
        on_device, mesh=mesh, in_specs=placed, out_specs=P("occ", ("int", "red")), check_vma=False
    )
```

```python
import functools

import jax
import jax.numpy as jnp
from jax import lax
from jax.experimental import pallas as pl
from jax.experimental.pallas import tpu as pltpu
from jax.sharding import PartitionSpec as P

MESH = pl.DeviceIdType.MESH
F32, BF16, I32 = jnp.float32, jnp.bfloat16, jnp.int32

LANES = 128
CHUNK = 400
GROUP = 1600
SLAB = 1280
HALF = 800
HALVES = ((0, 400), (400, 400))
PIECES = (HALVES, HALVES, ((0, 208), (208, 192), (400, 208), (608, 192)), HALVES)
OCC = 1024
DZ = (1, 3, 2, 0)
MIRROR = (1, 0, 2)
DIAG = 3


def dot(a, b, dims=((1,), (0,))):
    return lax.dot_general(a, b, (dims, ((), ())), preferred_element_type=F32)


def selections(z, given, kept, put):
    pair = lax.broadcasted_iota(I32, (1, LANES), 1)
    row = lax.broadcasted_iota(I32, (OCC, LANES), 0)

    def pairs_of(owner_is_lower):
        a = jnp.where(owner_is_lower, pair >> 4, pair >> 3)
        b = jnp.where(owner_is_lower, pair & 15, 8 + (pair & 7))
        return a, b

    for b in range(3):
        other = (z + DZ[b]) % 4
        if kept:
            p, q = pairs_of(z < other)
            put(b, jnp.where(row == p * 64 + other * 16 + q, 1.0, 0.0).astype(BF16))
        if given:
            p, q = pairs_of(other < z)
            put(4 + b, jnp.where(row == q * 64 + other * 16 + p, -1.0, 0.0).astype(BF16))
    if given:
        p = pair & 15
        q = (p + 1 + (pair >> 4)) & 15
        plus = jnp.where(pair < 120, p * 64 + z * 16 + q, -1)
        minus = jnp.where(pair < 120, q * 64 + z * 16 + p, -1)
        put(DIAG, (jnp.where(row == plus, 1.0, 0.0) - jnp.where(row == minus, 1.0, 0.0)).astype(BF16))


def store_kernel(ladder, out, sem):
    copy = pltpu.make_async_copy(ladder, out, sem)
    copy.start()
    copy.wait()


def kernel(
    t_hbm, v_hbm, out, tv, vv, slabs, sel, own, zs, zr, at, acc, total, rs, rr, lad, got,
    load_sem, zs_sem, zr_sem, as_sem, ar_sem, ds_sem, dr_sem, rs_sem, rr_sem, ls_sem, lr_sem,
):
    index, z, xh = lax.axis_index("int"), lax.axis_index("occ"), lax.axis_index("red")
    y, xl, c = index // 4, (index // 2) % 2, index % 2

    def device(dy=0, flip_x=0, flip_c=0, dz=0, flip_red=0):
        there = ((y + dy) % 4) * 4 + (xl ^ flip_x) * 2 + (c ^ flip_c)
        return {"int": there, "occ": (z + dz) % 4, "red": xh ^ flip_red}

    load_t = pltpu.make_async_copy(t_hbm, tv, load_sem.at[0])
    load_v = [
        pltpu.make_async_copy(v_hbm.at[:, n * SLAB : (n + 1) * SLAB], slabs.at[n % 2], load_sem.at[1 + n % 2])
        for n in range(4 * GROUP // SLAB)
    ]
    load_t.start()
    load_v[0].start()
    load_v[1].start()

    barrier = pltpu.get_barrier_semaphore()
    partners = [device(dy=1), device(dy=3), device(dz=1), device(dz=2), device(dz=3)]
    partners += [device(flip_x=1), device(flip_c=1), device(flip_red=1)]
    for partner in partners:
        pl.semaphore_signal(barrier, inc=1, device_id=partner, device_id_type=MESH)

    def turn(n):
        load_v[n].wait()

        def lanes(k, carry):
            first = pl.multiple_of(k * 128, 128)
            vv[pl.ds(n * SLAB + first, 128), :] = slabs[n % 2, :, pl.ds(first, 128)].T
            return carry

        lax.fori_loop(0, SLAB // 128, lanes, 0, unroll=2)
        if n + 2 < len(load_v):
            load_v[n + 2].start()

    sends = []

    def send(src, dst, send_sem, recv_sem, to):
        copy = pltpu.make_async_remote_copy(
            src_ref=src, dst_ref=dst, send_sem=send_sem, recv_sem=recv_sem, device_id=to, device_id_type=MESH
        )
        copy.start()
        sends.append(copy)

    def landed(ref, recv_sem):
        pltpu.make_async_copy(ref, ref, recv_sem).wait()

    def chunk(b, dy, rel, part=None):
        g = (y + dy) % 4
        start = CHUNK * ((xl ^ (rel >> 1)) * 2 + (c ^ (rel & 1)))
        first, rows = (0, CHUNK) if part is None else (part * 208, 208 - 16 * part)
        return at.at[b, g, pl.ds(pl.multiple_of(start + first, 16), rows), :]

    def pass_on(b, n, dy, rel, to_dy, to_rel, to):
        ref = chunk(b, dy, rel)
        send(ref, ref, as_sem.at[b, n], ar_sem.at[b, to_dy, to_rel], to)

    here = pl.ds(pl.multiple_of(CHUNK * (xl * 2 + c), 16), CHUNK)

    def to_next(b, rel):
        pass_on(b, 1 + 4 * (rel // 2), 0, rel, 3, rel, device(dy=1))

    def to_previous(b, rel):
        pass_on(b, 2 + 4 * (rel // 2), 0, rel, 1, rel, device(dy=3))

    def to_neighbours(b):
        pass_on(b, 0, 0, 0, 0, 2, device(flip_x=1))
        pass_on(b, 3, 0, 0, 0, 1, device(flip_c=1))

    def from_x(b, dy=0):
        landed(chunk(b, dy, 2), ar_sem.at[b, dy, 2])
        pass_on(b, 4 if dy == 0 else 8 + 2 * (dy - 1), dy, 2, dy, 3, device(flip_c=1))

    def share(b, dy, rel):
        landed(chunk(b, dy, rel), ar_sem.at[b, dy, rel])
        pass_on(b, 7 + 2 * (dy - 1) + rel // 2, dy, rel, dy, rel + 1, device(flip_c=1))

    def forward_next(b):
        pass_on(b, 13, 3, 0, 2, 0, device(dy=1))

    def forward_previous(b):
        pass_on(b, 14, 1, 2, 2, 2, device(dy=3))

    def across(dy):
        pass_on(DIAG, (13, 5, 6)[dy - 1], dy, 0, dy, 2, device(flip_x=1))

    def forward_diagonal(dy, k, to):
        ref = chunk(DIAG, dy, 0, k)
        send(ref, ref, ds_sem.at[k], dr_sem.at[k], to)

    def share_diagonal():
        for k in range(2):
            landed(chunk(DIAG, 2, 0, k), dr_sem.at[k])
        across(2)
        pass_on(DIAG, 9, 2, 0, 2, 1, device(flip_c=1))

    mine = xh * HALF
    theirs = (1 - xh) * HALF

    def multiply(b, dy):
        for rel in (1, 3):
            landed(chunk(b, dy, rel), ar_sem.at[b, dy, rel])
        g = (y + dy) % 4
        rows = pl.ds(pl.multiple_of(g * GROUP, 16), GROUP)
        product = dot(at[b, g].T, vv[rows, :])
        if dy == 0:
            acc[b] = product
        elif dy != 2:
            acc[b] += product
        else:
            total[b] = (acc[b] + product).T
            for h, (start, rows) in enumerate(PIECES[b]):
                rs[b, start : start + rows, :] = total[b, pl.ds(pl.multiple_of(theirs + start, 16), rows), :].astype(BF16)
                if b != DIAG:
                    reduce(b, h)

    def piece(ref, b, h):
        start, rows = PIECES[b][h]
        return ref.at[b, pl.ds(start, rows), :]

    def reduce(b, h):
        send(piece(rs, b, h), piece(rr, b, h), rs_sem.at[b, h], rr_sem.at[b, h], device(flip_red=1))

    def expand(blocks, h, first):
        start, rows = HALVES[h]
        half = slice(start, start + rows)
        for b in blocks:
            if b != DIAG:
                for k, (first_row, _) in enumerate(PIECES[b]):
                    if start <= first_row < start + rows:
                        landed(piece(got, b, k), lr_sem.at[b, k])
        parts = [lad[b, half, :] for b in blocks] + [got[b, half, :] for b in blocks if b != DIAG]
        places = list(blocks) + [4 + b for b in blocks if b != DIAG]
        parts = jnp.concatenate(parts, axis=1)
        for n in range(0, OCC, 256):
            where = jnp.concatenate([sel[b, n : n + 256, :] for b in places], axis=1)
            placed = dot(parts, where, ((1,), (1,)))
            if not first:
                placed += out[half, n : n + 256].astype(F32)
            out[half, n : n + 256] = placed.astype(BF16)

    def finish(b, h):
        landed(piece(rr, b, h), rr_sem.at[b, h])
        start, rows = PIECES[b][h]
        here = slice(start, start + rows)
        lad[b, here, :] = (total[b, pl.ds(pl.multiple_of(mine + start, 16), rows), :] + rr[b, here, :].astype(F32)).astype(BF16)
        if b != DIAG:
            m = MIRROR[b]
            there = got.at[m, pl.ds(start, rows), :]
            send(piece(lad, b, h), there, ls_sem.at[b, h], lr_sem.at[m, h], device(dz=DZ[b]))

    def put(b, places):
        sel[b] = places

    selections(z, True, False, put)
    load_t.wait()
    picked = dot(tv[...], jnp.concatenate([sel[b] for b in range(3, 7)], axis=1)).astype(BF16)
    at[DIAG, y, here, :] = picked[:, :LANES]
    for b in range(3):
        zs[b] = picked[:, (1 + b) * LANES : (2 + b) * LANES]
    pl.semaphore_wait(barrier, len(partners))
    def give(b):
        send(zs.at[b], zr.at[MIRROR[b]], zs_sem.at[b], zr_sem.at[MIRROR[b]], device(dz=DZ[b]))

    give(0)
    give(1)
    to_neighbours(DIAG)
    to_next(DIAG, 0)
    to_previous(DIAG, 0)

    selections(z, False, True, put)
    own[...] = dot(tv[...], jnp.concatenate([sel[b] for b in range(3)], axis=1))

    def antisymmetric(b):
        landed(zr.at[b], zr_sem.at[b])
        lanes = slice(b * LANES, (b + 1) * LANES)
        at[b, y, here, :] = (own[:, lanes] + zr[b].astype(F32)).astype(BF16)
        to_neighbours(b)

    turn(0)
    turn(1)
    share(DIAG, 3, 0)
    forward_diagonal(3, 0, device(dy=1))
    share(DIAG, 1, 0)
    forward_diagonal(1, 1, device(dy=3))
    from_x(DIAG)
    antisymmetric(0)
    to_next(0, 0)
    to_previous(0, 0)
    antisymmetric(1)
    to_next(1, 0)
    to_previous(1, 0)
    give(2)
    turn(2)
    turn(3)
    antisymmetric(2)
    across(1)
    across(3)
    share_diagonal()
    turn(4)
    from_x(0)
    to_previous(0, 2)
    to_next(0, 2)
    share(0, 3, 0)
    forward_next(0)
    share(0, 1, 0)
    multiply(DIAG, 0)
    multiply(0, 0)
    from_x(1)
    to_previous(1, 2)
    to_next(1, 2)
    share(1, 3, 0)
    forward_next(1)
    share(1, 1, 0)
    multiply(1, 0)
    from_x(2)
    to_next(2, 0)
    share(0, 1, 2)
    forward_previous(0)
    share(0, 3, 2)
    multiply(2, 0)
    multiply(0, 1)
    share(1, 1, 2)
    forward_previous(1)
    to_previous(2, 2)
    to_previous(2, 0)
    to_next(2, 2)
    share(0, 2, 0)
    from_x(DIAG, 1)
    multiply(0, 3)
    multiply(DIAG, 1)
    share(1, 3, 2)
    share(0, 2, 2)
    from_x(DIAG, 3)
    multiply(1, 1)
    multiply(0, 2)
    from_x(DIAG, 2)
    share(1, 2, 0)
    share(1, 2, 2)
    multiply(1, 3)
    multiply(DIAG, 3)
    share(2, 3, 0)
    forward_next(2)
    share(2, 1, 2)
    forward_previous(2)
    multiply(1, 2)
    multiply(DIAG, 2)
    reduce(DIAG, 0)
    share(2, 3, 2)
    share(2, 1, 0)
    multiply(2, 1)
    multiply(2, 3)
    share(2, 2, 0)
    share(2, 2, 2)
    finish(0, 0)
    finish(0, 1)
    multiply(2, 2)
    reduce(DIAG, 1)
    finish(1, 0)
    finish(1, 1)
    finish(2, 0)
    finish(2, 1)
    expand((0, 1), 0, True)
    expand((0, 1), 1, True)
    finish(2, 2)
    finish(2, 3)
    finish(DIAG, 0)
    expand((2, DIAG), 0, False)
    finish(DIAG, 1)
    expand((2, DIAG), 1, False)

    for copy in sends:
        copy.wait_send()


def on_device(amplitudes, integrals):
    dma = pltpu.SemaphoreType.DMA
    ladder = pl.pallas_call(
        kernel,
        out_shape=pltpu.VMEM((HALF, OCC), BF16),
        in_specs=[pl.BlockSpec(memory_space=pltpu.HBM)] * 2,
        out_specs=pl.BlockSpec(memory_space=pltpu.VMEM),
        scratch_shapes=[
            pltpu.VMEM((CHUNK, OCC), BF16),
            pltpu.VMEM((4 * GROUP, 2 * HALF), BF16),
            pltpu.VMEM((2, 2 * HALF, SLAB), BF16),
            pltpu.VMEM((7, OCC, LANES), BF16),
            pltpu.VMEM((CHUNK, 3 * LANES), F32),
            pltpu.VMEM((3, CHUNK, LANES), BF16),
            pltpu.VMEM((3, CHUNK, LANES), BF16),
            pltpu.VMEM((4, 4, GROUP, LANES), BF16),
            pltpu.VMEM((4, LANES, 2 * HALF), F32),
            pltpu.VMEM((4, 2 * HALF, LANES), F32),
            pltpu.VMEM((4, HALF, LANES), BF16),
            pltpu.VMEM((4, HALF, LANES), BF16),
            pltpu.VMEM((4, HALF, LANES), BF16),
            pltpu.VMEM((3, HALF, LANES), BF16),
            dma((3,)), dma((3,)), dma((3,)), dma((4, 15)), dma((4, 4, 4)), dma((2,)), dma((2,)),
            dma((4, 4)), dma((4, 4)), dma((3, 4)), dma((3, 4)),
        ],
        compiler_params=pltpu.CompilerParams(
            collective_id=0, has_side_effects=True, vmem_limit_bytes=117 * 2**19
        ),
        name="ladder",
    )(amplitudes.T, integrals.T)
    ladder = pl.pallas_call(
        store_kernel,
        out_shape=jax.ShapeDtypeStruct((HALF, OCC), BF16),
        in_specs=[pl.BlockSpec(memory_space=pltpu.VMEM)],
        out_specs=pl.BlockSpec(memory_space=pltpu.HBM),
        scratch_shapes=[pltpu.SemaphoreType.DMA],
        name="store",
    )(pltpu.with_memory_space_constraint(ladder, pltpu.VMEM))
    return ladder.T


def solution(mesh):
    placed = (P("occ", ("red", "int")), P("red", "int"))
    return jax.shard_map(
        on_device, mesh=mesh, in_specs=placed, out_specs=P("occ", ("int", "red")), check_vma=False
    )
```

```python
import jax
import jax.numpy as jnp
from jax import lax
from jax.experimental import pallas as pl
from jax.experimental.pallas import tpu as pltpu
from jax.sharding import PartitionSpec as P

MESH = pl.DeviceIdType.MESH
F32, BF16, I32 = jnp.float32, jnp.bfloat16, jnp.int32

LANES = 128
CHUNK = 400
GROUP = 1600
SLAB = 1280
HALF = 800
HALVES = ((0, 400), (400, 400))
PIECES = (HALVES, HALVES, ((0, 208), (208, 192), (400, 208), (608, 192)), HALVES)
OCC = 1024
DZ = (1, 3, 2, 0)
MIRROR = (1, 0, 2)
DIAG = 3


def dot(a, b, dims=((1,), (0,))):
    return lax.dot_general(a, b, (dims, ((), ())), preferred_element_type=F32)


def selections(z, given, kept, put):
    pair = lax.broadcasted_iota(I32, (1, LANES), 1)
    row = lax.broadcasted_iota(I32, (OCC, LANES), 0)

    def pairs_of(owner_is_lower):
        a = jnp.where(owner_is_lower, pair >> 4, pair >> 3)
        b = jnp.where(owner_is_lower, pair & 15, 8 + (pair & 7))
        return a, b

    for b in range(3):
        other = (z + DZ[b]) % 4
        if kept:
            p, q = pairs_of(z < other)
            put(b, jnp.where(row == p * 64 + other * 16 + q, 1.0, 0.0).astype(BF16))
        if given:
            p, q = pairs_of(other < z)
            put(4 + b, jnp.where(row == q * 64 + other * 16 + p, -1.0, 0.0).astype(BF16))
    if given:
        p = pair & 15
        q = (p + 1 + (pair >> 4)) & 15
        plus = jnp.where(pair < 120, p * 64 + z * 16 + q, -1)
        minus = jnp.where(pair < 120, q * 64 + z * 16 + p, -1)
        put(DIAG, (jnp.where(row == plus, 1.0, 0.0) - jnp.where(row == minus, 1.0, 0.0)).astype(BF16))


def store_kernel(ladder, out, sem):
    copy = pltpu.make_async_copy(ladder, out, sem)
    copy.start()
    copy.wait()


def kernel(
    t_hbm, v_hbm, out, tv, vv, slabs, sel, own, zs, zr, at, acc, total, rs, rr, lad, got,
    load_sem, zs_sem, zr_sem, as_sem, ar_sem, ds_sem, dr_sem, rs_sem, rr_sem, ls_sem, lr_sem,
):
    index, z, xh = lax.axis_index("int"), lax.axis_index("occ"), lax.axis_index("red")
    y, xl, c = index // 4, (index // 2) % 2, index % 2

    def device(dy=0, flip_x=0, flip_c=0, dz=0, flip_red=0):
        there = ((y + dy) % 4) * 4 + (xl ^ flip_x) * 2 + (c ^ flip_c)
        return {"int": there, "occ": (z + dz) % 4, "red": xh ^ flip_red}

    load_t = pltpu.make_async_copy(t_hbm, tv, load_sem.at[0])
    load_v = [
        pltpu.make_async_copy(v_hbm.at[:, n * SLAB : (n + 1) * SLAB], slabs.at[n % 4], load_sem.at[1 + n % 4])
        for n in range(4 * GROUP // SLAB)
    ]
    load_t.start()
    for load in load_v[:4]:
        load.start()

    barrier = pltpu.get_barrier_semaphore()
    partners = [device(dy=1), device(dy=3), device(dz=1), device(dz=2), device(dz=3)]
    partners += [device(flip_x=1), device(flip_c=1), device(flip_red=1)]
    for partner in partners:
        pl.semaphore_signal(barrier, inc=1, device_id=partner, device_id_type=MESH)

    def turn(n):
        load_v[n].wait()

        def lanes(k, carry):
            first = pl.multiple_of(k * 128, 128)
            vv[pl.ds(n * SLAB + first, 128), :] = slabs[n % 4, :, pl.ds(first, 128)].T
            return carry

        lax.fori_loop(0, SLAB // 128, lanes, 0, unroll=2)
        if n + 4 < len(load_v):
            load_v[n + 4].start()

    sends = []

    def send(src, dst, send_sem, recv_sem, to):
        copy = pltpu.make_async_remote_copy(
            src_ref=src, dst_ref=dst, send_sem=send_sem, recv_sem=recv_sem, device_id=to, device_id_type=MESH
        )
        copy.start()
        sends.append(copy)

    def landed(ref, recv_sem):
        pltpu.make_async_copy(ref, ref, recv_sem).wait()

    def chunk(b, dy, rel, part=None):
        g = (y + dy) % 4
        start = CHUNK * ((xl ^ (rel >> 1)) * 2 + (c ^ (rel & 1)))
        first, rows = (0, CHUNK) if part is None else (part * 208, 208 - 16 * part)
        return at.at[b, g, pl.ds(pl.multiple_of(start + first, 16), rows), :]

    def pass_on(b, n, dy, rel, to_dy, to_rel, to):
        ref = chunk(b, dy, rel)
        send(ref, ref, as_sem.at[b, n], ar_sem.at[b, to_dy, to_rel], to)

    here = pl.ds(pl.multiple_of(CHUNK * (xl * 2 + c), 16), CHUNK)

    def to_next(b, rel):
        pass_on(b, 1 + 4 * (rel // 2), 0, rel, 3, rel, device(dy=1))

    def to_previous(b, rel):
        pass_on(b, 2 + 4 * (rel // 2), 0, rel, 1, rel, device(dy=3))

    def to_neighbours(b):
        pass_on(b, 0, 0, 0, 0, 2, device(flip_x=1))
        pass_on(b, 3, 0, 0, 0, 1, device(flip_c=1))

    def from_x(b, dy=0):
        landed(chunk(b, dy, 2), ar_sem.at[b, dy, 2])
        pass_on(b, 4 if dy == 0 else 8 + 2 * (dy - 1), dy, 2, dy, 3, device(flip_c=1))

    def share(b, dy, rel):
        landed(chunk(b, dy, rel), ar_sem.at[b, dy, rel])
        pass_on(b, 7 + 2 * (dy - 1) + rel // 2, dy, rel, dy, rel + 1, device(flip_c=1))

    def forward_next(b):
        pass_on(b, 13, 3, 0, 2, 0, device(dy=1))

    def forward_previous(b):
        pass_on(b, 14, 1, 2, 2, 2, device(dy=3))

    def across(dy):
        pass_on(DIAG, (13, 5, 6)[dy - 1], dy, 0, dy, 2, device(flip_x=1))

    def forward_diagonal(dy, k, to):
        ref = chunk(DIAG, dy, 0, k)
        send(ref, ref, ds_sem.at[k], dr_sem.at[k], to)

    def share_diagonal():
        for k in range(2):
            landed(chunk(DIAG, 2, 0, k), dr_sem.at[k])
        across(2)
        pass_on(DIAG, 9, 2, 0, 2, 1, device(flip_c=1))

    mine = xh * HALF
    theirs = (1 - xh) * HALF

    def multiply(b, dy):
        for rel in (1, 3):
            landed(chunk(b, dy, rel), ar_sem.at[b, dy, rel])
        g = (y + dy) % 4
        rows = pl.ds(pl.multiple_of(g * GROUP, 16), GROUP)
        product = dot(at[b, g].T, vv[rows, :])
        if dy == 0:
            acc[b] = product
        elif dy != 2:
            acc[b] += product
        else:
            total[b] = (acc[b] + product).T
            for h, (start, rows) in enumerate(PIECES[b]):
                rs[b, start : start + rows, :] = total[b, pl.ds(pl.multiple_of(theirs + start, 16), rows), :].astype(BF16)
                if b != DIAG:
                    reduce(b, h)

    def piece(ref, b, h):
        start, rows = PIECES[b][h]
        return ref.at[b, pl.ds(start, rows), :]

    def reduce(b, h):
        send(piece(rs, b, h), piece(rr, b, h), rs_sem.at[b, h], rr_sem.at[b, h], device(flip_red=1))

    def expand(blocks, h, first):
        start, rows = HALVES[h]
        half = slice(start, start + rows)
        for b in blocks:
            if b != DIAG:
                for k, (first_row, _) in enumerate(PIECES[b]):
                    if start <= first_row < start + rows:
                        landed(piece(got, b, k), lr_sem.at[b, k])
        parts = [lad[b, half, :] for b in blocks] + [got[b, half, :] for b in blocks if b != DIAG]
        places = list(blocks) + [4 + b for b in blocks if b != DIAG]
        parts = jnp.concatenate(parts, axis=1)
        for n in range(0, OCC, 256):
            where = jnp.concatenate([sel[b, n : n + 256, :] for b in places], axis=1)
            placed = dot(parts, where, ((1,), (1,)))
            if not first:
                placed += out[half, n : n + 256].astype(F32)
            out[half, n : n + 256] = placed.astype(BF16)

    def finish(b, h):
        landed(piece(rr, b, h), rr_sem.at[b, h])
        start, rows = PIECES[b][h]
        here = slice(start, start + rows)
        lad[b, here, :] = (total[b, pl.ds(pl.multiple_of(mine + start, 16), rows), :] + rr[b, here, :].astype(F32)).astype(BF16)
        if b != DIAG:
            m = MIRROR[b]
            there = got.at[m, pl.ds(start, rows), :]
            send(piece(lad, b, h), there, ls_sem.at[b, h], lr_sem.at[m, h], device(dz=DZ[b]))

    def put(b, places):
        sel[b] = places

    selections(z, True, False, put)
    load_t.wait()
    picked = dot(tv[...], jnp.concatenate([sel[b] for b in range(3, 7)], axis=1)).astype(BF16)
    at[DIAG, y, here, :] = picked[:, :LANES]
    for b in range(3):
        zs[b] = picked[:, (1 + b) * LANES : (2 + b) * LANES]
    pl.semaphore_wait(barrier, len(partners))
    def give(b):
        send(zs.at[b], zr.at[MIRROR[b]], zs_sem.at[b], zr_sem.at[MIRROR[b]], device(dz=DZ[b]))

    give(0)
    give(1)
    to_neighbours(DIAG)
    to_next(DIAG, 0)
    to_previous(DIAG, 0)

    selections(z, False, True, put)
    own[...] = dot(tv[...], jnp.concatenate([sel[b] for b in range(3)], axis=1))

    def antisymmetric(b):
        landed(zr.at[b], zr_sem.at[b])
        lanes = slice(b * LANES, (b + 1) * LANES)
        at[b, y, here, :] = (own[:, lanes] + zr[b].astype(F32)).astype(BF16)
        to_neighbours(b)

    turn(0)
    turn(1)
    share(DIAG, 3, 0)
    forward_diagonal(3, 0, device(dy=1))
    share(DIAG, 1, 0)
    forward_diagonal(1, 1, device(dy=3))
    from_x(DIAG)
    antisymmetric(0)
    to_next(0, 0)
    to_previous(0, 0)
    antisymmetric(1)
    to_next(1, 0)
    to_previous(1, 0)
    give(2)
    turn(2)
    turn(3)
    turn(4)
    antisymmetric(2)
    across(1)
    across(3)
    share_diagonal()
    from_x(0)
    to_previous(0, 2)
    to_next(0, 2)
    share(0, 3, 0)
    forward_next(0)
    share(0, 1, 0)
    multiply(DIAG, 0)
    multiply(0, 0)
    from_x(1)
    to_previous(1, 2)
    to_next(1, 2)
    share(1, 3, 0)
    forward_next(1)
    share(1, 1, 0)
    multiply(1, 0)
    from_x(2)
    to_next(2, 0)
    share(0, 1, 2)
    forward_previous(0)
    share(0, 3, 2)
    multiply(0, 1)
    share(1, 1, 2)
    forward_previous(1)
    to_previous(2, 2)
    to_previous(2, 0)
    to_next(2, 2)
    share(0, 2, 0)
    from_x(DIAG, 1)
    multiply(0, 3)
    multiply(DIAG, 1)
    share(1, 3, 2)
    share(0, 2, 2)
    from_x(DIAG, 3)
    multiply(1, 1)
    multiply(0, 2)
    multiply(2, 0)
    from_x(DIAG, 2)
    share(1, 2, 0)
    share(1, 2, 2)
    multiply(1, 3)
    multiply(DIAG, 3)
    share(2, 3, 0)
    forward_next(2)
    share(2, 1, 2)
    forward_previous(2)
    multiply(1, 2)
    multiply(DIAG, 2)
    reduce(DIAG, 0)
    share(2, 3, 2)
    share(2, 1, 0)
    multiply(2, 1)
    multiply(2, 3)
    share(2, 2, 0)
    share(2, 2, 2)
    finish(0, 0)
    finish(0, 1)
    multiply(2, 2)
    reduce(DIAG, 1)
    finish(1, 0)
    finish(1, 1)
    finish(2, 0)
    finish(2, 1)
    expand((0, 1), 0, True)
    expand((0, 1), 1, True)
    finish(2, 2)
    finish(2, 3)
    finish(DIAG, 0)
    expand((2, DIAG), 0, False)
    finish(DIAG, 1)
    expand((2, DIAG), 1, False)

    for copy in sends:
        copy.wait_send()


def on_device(amplitudes, integrals):
    dma = pltpu.SemaphoreType.DMA
    ladder = pl.pallas_call(
        kernel,
        out_shape=pltpu.VMEM((HALF, OCC), BF16),
        in_specs=[pl.BlockSpec(memory_space=pltpu.HBM)] * 2,
        out_specs=pl.BlockSpec(memory_space=pltpu.VMEM),
        scratch_shapes=[
            pltpu.VMEM((CHUNK, OCC), BF16),
            pltpu.VMEM((4 * GROUP, 2 * HALF), BF16),
            pltpu.VMEM((4, 2 * HALF, SLAB), BF16),
            pltpu.VMEM((7, OCC, LANES), BF16),
            pltpu.VMEM((CHUNK, 3 * LANES), F32),
            pltpu.VMEM((3, CHUNK, LANES), BF16),
            pltpu.VMEM((3, CHUNK, LANES), BF16),
            pltpu.VMEM((4, 4, GROUP, LANES), BF16),
            pltpu.VMEM((4, LANES, 2 * HALF), F32),
            pltpu.VMEM((4, 2 * HALF, LANES), F32),
            pltpu.VMEM((4, HALF, LANES), BF16),
            pltpu.VMEM((4, HALF, LANES), BF16),
            pltpu.VMEM((4, HALF, LANES), BF16),
            pltpu.VMEM((3, HALF, LANES), BF16),
            dma((5,)), dma((3,)), dma((3,)), dma((4, 15)), dma((4, 4, 4)), dma((2,)), dma((2,)),
            dma((4, 4)), dma((4, 4)), dma((3, 4)), dma((3, 4)),
        ],
        compiler_params=pltpu.CompilerParams(
            collective_id=0, has_side_effects=True, vmem_limit_bytes=117 * 2**19
        ),
        name="ladder",
    )(amplitudes.T, integrals.T)
    ladder = pl.pallas_call(
        store_kernel,
        out_shape=jax.ShapeDtypeStruct((HALF, OCC), BF16),
        in_specs=[pl.BlockSpec(memory_space=pltpu.VMEM)],
        out_specs=pl.BlockSpec(memory_space=pltpu.HBM),
        scratch_shapes=[pltpu.SemaphoreType.DMA],
        name="store",
    )(pltpu.with_memory_space_constraint(ladder, pltpu.VMEM))
    return ladder.T


def solution(mesh):
    placed = (P("occ", ("red", "int")), P("red", "int"))
    return jax.shard_map(
        on_device, mesh=mesh, in_specs=placed, out_specs=P("occ", ("int", "red")), check_vma=False
    )
```
